32 devices in a mesh: fsdp: 4 (over z), rep: 8 (over y, x, core).
Axes of the slice: x: 2, y: 2, z: 4, core: 2. Of those that a mesh axis runs over, the one named last changes fastest.
Arguments:
- gradients: bfloat16 [8, 8, 360, 3584], P('rep', None, 'fsdp'), may hold values from -6 to 6
- momentum: float32 [8, 360, 3584], P('rep', 'fsdp')
- offsets: int32 [8, 5], P('rep'), may hold values from 0 to 288, as said below
Outputs:
- kept_state: float32 [8, 360, 3584], P('rep', 'fsdp')
- update: bfloat16 [8, 360, 3584], P('rep', 'fsdp')
The draws below stay inside these ranges and needn't reach their ends.
Inputs may be any that keep to these rules, and one draw needn't show every extreme that they name: offsets[k, 0] = 0 and offsets[k, 4] = 288; offsets never fall; every index of fsdp holds between 54 and 90 rows of each matrix, and in every matrix some index holds exactly 90.
All inputs are finite; a program needn't handle non-finite values.
Results may differ from the reference program's by a relative error of at most 0.024.
Values may be sent and summed in bfloat16 or wider, within the bound.
No kernel may reach another device: no remote copies, remote signals or barrier semaphores. Data moves between devices by JAX's collectives and lax.ppermute only.
A program may use at most 64 MiB of HBM per device.

```python
import math
import jax
import jax.numpy as jnp
from jax import lax

D = 3584
ROWS = 288
ITERS = 3
CAP = 90
MATS = 8
N_FSDP = 4
N_REP = 8


def draw_momentum(key, part):
    key = jax.random.fold_in(key, 5)
    key_values, key_rows, key_cols = jax.random.split(key, 3)
    shape = (MATS, N_FSDP * CAP, D)
    row_scale = jnp.exp(jax.random.uniform(key_rows, (MATS, N_FSDP * CAP, 1), jnp.float32) * math.log(10.0))
    col_scale = jnp.exp(jax.random.uniform(key_cols, (MATS, 1, D), jnp.float32) * math.log(10.0))
    values = jax.random.normal(key_values, shape, jnp.float32) * row_scale * col_scale * 0.05
    return values.astype(jnp.float32)


def draw_offsets(key, part):
    key = jax.random.fold_in(key, 11)
    share = ROWS // N_FSDP
    spread = CAP - share

    def one_matrix(matrix_key):
        key_order, key_sizes = jax.random.split(matrix_key, 2)
        order = jax.random.permutation(key_order, N_FSDP)
        paired = jax.random.randint(key_sizes, (N_FSDP // 2,), 0, spread + 1).astype(jnp.int32)
        paired = paired.at[0].set(spread)
        deltas = jnp.stack([paired, -paired], axis=1).reshape(N_FSDP)
        placed = jnp.zeros((N_FSDP,), jnp.int32).at[order].set(deltas)
        counts = share + placed
        return jnp.concatenate([jnp.zeros((1,), jnp.int32), jnp.cumsum(counts).astype(jnp.int32)])
    return jax.vmap(one_matrix)(jax.random.split(key, MATS))


def with_spikes(drawn, stream_key, source, target, shards_of, factor):
    owner, partner = [(jnp.arange(drawn.shape[dim]) // (drawn.shape[dim] // shards_of)).reshape([-1 if axis == dim else 1 for axis in range(drawn.ndim)]) for dim in (source, target)]
    chosen = jax.random.permutation(stream_key, shards_of)[partner]
    strong = (owner == chosen) | (owner == (partner + shards_of // 2) % shards_of)
    return jnp.where(strong, factor * drawn, drawn)


def steps_of(own_key, shape, shards, smallest, top_value):
    def one(dim, parts):
        draws = jax.random.uniform(jax.random.fold_in(jax.random.fold_in(own_key, 6), dim), (parts,), jnp.float32, smallest / len(shards), top_value / len(shards))
        return jnp.repeat(jnp.exp(draws), shape[dim] // parts).reshape((-1,) + (1,) * (len(shape) - dim - 1))

    loudness = one(*shards[0])
    for cut in shards[1:]:
        loudness = loudness * one(*cut)
    return loudness


def gaussian_with(stream_key, shape, width, limit, cuts, heavy, kind=jnp.bfloat16):
    drawn = width * jax.random.normal(stream_key, shape, jnp.float32)
    if cuts:
        drawn = drawn * steps_of(stream_key, shape, cuts, -0.22, 0.18)
    return jnp.clip(with_spikes(drawn, jax.random.fold_in(stream_key, 3), *heavy), -limit, limit).astype(kind)


def setup_inputs(seed: int = 0) -> dict:
    arg_keys = jax.random.split(jax.random.key(seed), 4)
    return {
        "gradients": gaussian_with(arg_keys[0], (N_REP, MATS, N_FSDP * CAP, D), 1.0, 6.0, ((0, 8), (2, 4)), (0, 1, 8, 2.0)),
        "momentum": draw_momentum(jax.random.fold_in(arg_keys[3], 71), 0),
        "offsets": draw_offsets(jax.random.fold_in(arg_keys[3], 71), 0),
    }


momentum_rate = 0.95
coef_a = 3.4445
coef_b = -4.775
coef_c = 2.0315

def orthogonalize(matrix):
    values = matrix.astype(jnp.float32)
    frob_norm = jnp.sqrt(jnp.sum(values * values))
    iterate = (values / (frob_norm + 1e-07)).astype(jnp.bfloat16)
    for iteration in range(ITERS):
        gram_matrix = lax.dot_general(iterate, iterate, (((1,), (1,)), ((), ())), preferred_element_type=jnp.float32).astype(jnp.bfloat16)
        gram_square = jnp.dot(gram_matrix, gram_matrix, preferred_element_type=jnp.float32)
        polynomial = (coef_b * gram_matrix.astype(jnp.float32) + coef_c * gram_square).astype(jnp.bfloat16)
        iterate = (coef_a * iterate.astype(jnp.float32) + jnp.dot(polynomial, iterate, preferred_element_type=jnp.float32)).astype(jnp.bfloat16)
    return iterate

def row_index(bounds):
    position = jnp.arange(ROWS, dtype=jnp.int32)
    holder = lax.optimization_barrier(jnp.sum((bounds[None, 1:N_FSDP] <= position[:, None]).astype(jnp.int32), axis=1))
    return holder * CAP + position - jnp.take(bounds, holder)

def reference(gradients, momentum, offsets):
    slot_rows = jnp.arange(N_FSDP * CAP, dtype=jnp.int32)
    holder_of_slot = slot_rows // CAP
    slot_index = slot_rows % CAP

    def per_matrix(number):
        replica_terms = lax.dynamic_index_in_dim(gradients, number, 1, keepdims=False)
        mean_grad = lax.optimization_barrier(jnp.sum(replica_terms.astype(jnp.float32), axis=0)) / N_REP
        bounds = lax.dynamic_index_in_dim(offsets, number, 0, keepdims=False)
        counts = bounds[1:] - bounds[:-1]
        live_slot = slot_index < jnp.take(counts, holder_of_slot)
        old_state = lax.dynamic_index_in_dim(momentum, number, 0, keepdims=False)
        buffer_new = momentum_rate * old_state + mean_grad
        nesterov = (mean_grad + momentum_rate * buffer_new).astype(jnp.bfloat16)
        full_matrix = jnp.take(nesterov, row_index(bounds), axis=0)
        orthogonal = orthogonalize(full_matrix)
        source = jnp.clip(jnp.take(bounds, holder_of_slot) + slot_index, 0, ROWS - 1)
        placed = jnp.take(orthogonal, source, axis=0).astype(jnp.float32) * math.sqrt(D)
        update = jnp.where(live_slot[:, None], placed, 0.0).astype(jnp.bfloat16)
        kept_state = jnp.where(live_slot[:, None], buffer_new, 0.0)
        return (kept_state, update)
    kept_state, update = lax.map(per_matrix, jnp.arange(MATS, dtype=jnp.int32))
    return (kept_state, update)
```

```python
import functools
import math

import jax
import jax.numpy as jnp
from jax import lax
from jax.experimental import pallas as pl
from jax.experimental.pallas import tpu as pltpu
from jax.sharding import PartitionSpec as P

ITERS = 3
CHUNKS = 2

momentum_rate = 0.95
coef_a = 3.4445
coef_b = -4.775
coef_c = 2.0315

AXES = ("fsdp", "rep")
VMEM_LIMIT = 32 * 1024 * 1024
bf16 = jnp.bfloat16
f32 = jnp.float32


def split_kernel(mats, cap, me_ref, x_ref, keep_ref, send_ref):
    me = me_ref[0]
    rows = min(256 // mats, cap)
    half = mats // 2
    padded = keep_ref.shape[1]
    size = rows * mats
    out_row = lax.broadcasted_iota(jnp.int32, (size, size), 0)
    in_row = lax.broadcasted_iota(jnp.int32, (size, size), 1)
    place = out_row // rows
    within = out_row - place * rows
    j = jnp.where(place < half, 2 * place, 2 * (place - half) + 1)
    matrix = jnp.bitwise_xor(j, me)
    blocks = -(-cap // rows)
    for block in range(blocks):
        first = block * rows
        start = min(first, cap - rows)
        source = (within + (first - start)) * mats + matrix
        chosen = (in_row == source) & (within < cap - first)
        moved = jnp.dot(
            chosen.astype(f32).astype(bf16),
            x_ref[start * mats : start * mats + size, :],
            preferred_element_type=f32,
        )
        moved = moved.reshape(mats, rows, moved.shape[1])
        here = min(rows, padded - first)
        keep_ref[:, first : first + here, :] = moved[:half, :here].astype(bf16)
        send_ref[:, first : first + here, :] = moved[half:, :here].astype(bf16)
    done = blocks * rows
    if done < padded:
        zeros = jnp.zeros((half, padded - done, keep_ref.shape[2]), bf16)
        keep_ref[:, done:, :] = zeros
        send_ref[:, done:, :] = zeros


def split(me, flat, mats, cap, padded, first, width):
    half = mats // 2
    out = jax.ShapeDtypeStruct((half, padded, width), bf16)
    tile = 128
    while tile * 2 <= 512 and width % (tile * 2) == 0:
        tile *= 2
    offset = first // tile
    return pl.pallas_call(
        functools.partial(split_kernel, mats, cap),
        grid=(width // tile,),
        out_shape=(out, out),
        in_specs=[
            pl.BlockSpec(memory_space=pltpu.SMEM),
            pl.BlockSpec((flat.shape[0], tile), lambda i: (0, i + offset)),
        ],
        out_specs=[pl.BlockSpec((half, padded, tile), lambda i: (0, 0, i))] * 2,
        compiler_params=pltpu.CompilerParams(vmem_limit_bytes=VMEM_LIMIT),
        cost_estimate=pl.CostEstimate(
            flops=2 * flat.shape[0] * 256 * width,
            bytes_accessed=4 * flat.shape[0] * width,
            transcendentals=0,
        ),
    )(me, flat)


def dot(left, right):
    return jnp.dot(left, right, preferred_element_type=f32)


def gram_of(parts, stack_ref):
    rows = parts[0].shape[0]
    for i, part in enumerate(parts):
        stack_ref[i * rows : (i + 1) * rows, :] = part[...]
    return lax.dot_general(
        stack_ref[...], stack_ref[...], (((1,), (1,)), ((), ())), preferred_element_type=f32
    )


def gram_kernel(*refs):
    *parts, out_ref, stack_ref = refs
    out_ref[...] = gram_of(parts, stack_ref)


def two(value):
    high = value.astype(bf16)
    return high, (value - high.astype(f32)).astype(bf16)


def chain_kernel(width, earlier, *refs):
    sums, parts = refs[:earlier], refs[earlier:-4]
    high_ref, low_ref, alpha_ref, stack_ref = refs[-4:]
    gram = gram_of(parts, stack_ref)
    for earlier_ref in sums:
        gram = gram + earlier_ref[...]
    size = gram.shape[0]
    diagonal = lax.broadcasted_iota(jnp.int32, (size, size), 0) == lax.broadcasted_iota(
        jnp.int32, (size, size), 1
    )
    trace = jnp.sum(jnp.where(diagonal, gram, 0.0), keepdims=True)
    scale = 1.0 / (jnp.sqrt(trace) + 1e-07)
    gram = (gram * scale) * scale
    rest = None
    power = 1.0
    for iteration in range(ITERS):
        rounded = gram.astype(bf16)
        square = dot(rounded, rounded)
        poly = (coef_b * rounded.astype(f32) + coef_c * square).astype(bf16)
        if rest is None:
            rest = poly.astype(f32)
        else:
            rest_high, rest_low = two(rest)
            rest = (
                coef_a * rest
                + power * poly.astype(f32)
                + (dot(poly, rest_high) + dot(poly, rest_low))
            )
        power = power * coef_a
        if iteration < ITERS - 1:
            gram_high, gram_low = two(gram)
            left = coef_a * gram + (dot(poly, gram_high) + dot(poly, gram_low))
            left_high, left_low = two(left)
            gram = coef_a * left + (dot(left_high, poly) + dot(left_low, poly))
    scale = scale * math.sqrt(width)
    high, low = two(rest * scale)
    high_ref[...] = high
    low_ref[...] = low
    alpha_ref[...] = jnp.broadcast_to(scale * power, alpha_ref.shape)


def apply_kernel(groups, *refs):
    high_ref, low_ref, alpha_ref = refs[:3]
    parts, outs, stack_ref = refs[3 : 3 + groups], refs[3 + groups : -1], refs[-1]
    rows = parts[0].shape[0]
    for i, part in enumerate(parts):
        stack_ref[i * rows : (i + 1) * rows, :] = part[...]
    alpha = alpha_ref[0:1, 0:1]
    stack = stack_ref[...]
    result = dot(high_ref[...], stack) + dot(low_ref[...], stack)
    result = result + alpha * stack.astype(f32)
    for i, out in enumerate(outs):
        out[...] = result[i * rows : (i + 1) * rows, :].astype(bf16)


def whole(count):
    return [pl.BlockSpec(memory_space=pltpu.VMEM)] * count


def gram_call(parts):
    size = len(parts) * parts[0].shape[0]
    width = parts[0].shape[1]
    return pl.pallas_call(
        gram_kernel,
        out_shape=jax.ShapeDtypeStruct((size, size), f32),
        in_specs=whole(len(parts)),
        out_specs=pl.BlockSpec(memory_space=pltpu.VMEM),
        scratch_shapes=[pltpu.VMEM((size, width), bf16)],
        compiler_params=pltpu.CompilerParams(vmem_limit_bytes=VMEM_LIMIT),
        cost_estimate=pl.CostEstimate(
            flops=2 * size * size * width, bytes_accessed=2 * size * width, transcendentals=0
        ),
    )(*parts)


def chain_call(full_width, sums, parts):
    size = len(parts) * parts[0].shape[0]
    width = parts[0].shape[1]
    return pl.pallas_call(
        functools.partial(chain_kernel, full_width, len(sums)),
        out_shape=(
            jax.ShapeDtypeStruct((size, size), bf16),
            jax.ShapeDtypeStruct((size, size), bf16),
            jax.ShapeDtypeStruct((8, 128), f32),
        ),
        in_specs=whole(len(sums) + len(parts)),
        out_specs=whole(3),
        scratch_shapes=[pltpu.VMEM((size, width), bf16)],
        compiler_params=pltpu.CompilerParams(vmem_limit_bytes=VMEM_LIMIT),
        cost_estimate=pl.CostEstimate(
            flops=2 * size * size * (width + 14 * size),
            bytes_accessed=2 * size * width,
            transcendentals=0,
        ),
    )(*sums, *parts)


def apply_call(factors, parts):
    groups = len(parts)
    rows, width = parts[0].shape
    size = groups * rows
    return pl.pallas_call(
        functools.partial(apply_kernel, groups),
        out_shape=tuple(jax.ShapeDtypeStruct((rows, width), bf16) for _ in range(groups)),
        in_specs=whole(3 + groups),
        out_specs=whole(groups),
        scratch_shapes=[pltpu.VMEM((size, width), bf16)],
        compiler_params=pltpu.CompilerParams(vmem_limit_bytes=VMEM_LIMIT),
        cost_estimate=pl.CostEstimate(
            flops=4 * size * size * width, bytes_accessed=4 * size * width, transcendentals=0
        ),
    )(*factors, *parts)


def per_device(groups, replicas, gradients, momentum, offsets):
    _, mats, cap, width = gradients.shape
    padded = -(-cap // 16) * 16
    fsdp = lax.axis_index("fsdp")
    me = lax.axis_index("rep")
    bits = [1 << i for i in range(replicas.bit_length() - 1)]

    def swap(value, bit):
        pairs = [(f * replicas + r, f * replicas + (r ^ bit)) for f in range(groups) for r in range(replicas)]
        return lax.ppermute(value, AXES, pairs)

    def owner(r):
        return (groups - 1) // 2 + (r & 1)

    def sources(r):
        return [f for f in range(groups) if f != owner(r)]

    def to_owner(value, k):
        pairs = [(sources(r)[k] * replicas + r, owner(r) * replicas + r) for r in range(replicas)]
        return lax.ppermute(value, AXES, pairs)

    def from_owner(value, k):
        pairs = [(owner(r) * replicas + r, sources(r)[k] * replicas + r) for r in range(replicas)]
        return lax.ppermute(value, AXES, pairs)

    flat = jnp.transpose(gradients[0], (1, 0, 2)).reshape(cap * mats, width)
    me_array = me.astype(jnp.int32).reshape(1)

    def total(terms, places):
        return sum(jnp.stack([term[p] for p in places]).astype(f32) for term in terms)

    part = width // (2 * CHUNKS)
    orders = [bits[1:], bits[1:][::-1]]
    state = {}
    for chunk in range(CHUNKS):
        for side in range(2):
            first = (chunk * 2 + side) * part
            keep, send = split(me_array, flat, mats, cap, padded, first, part)
            state[chunk, side] = ([2 * i for i in range(mats // 2)], [keep, swap(send, 1)])
    for level in range(len(bits) - 1):
        for chunk in range(CHUNKS):
            for side in range(2):
                js, terms = state[chunk, side]
                bit = orders[side][level]
                away = [p for p, j in enumerate(js) if j & bit]
                stay = [p for p, j in enumerate(js) if not j & bit]
                got = swap(total(terms, away).astype(bf16), bit)
                terms = [jnp.stack([term[p] for p in stay]) for term in terms] + [got]
                state[chunk, side] = ([js[p] for p in stay], terms)

    bounds = offsets[0]
    count = lax.dynamic_index_in_dim(bounds, fsdp + 1, 0, keepdims=False) - lax.dynamic_index_in_dim(
        bounds, fsdp, 0, keepdims=False
    )
    live = (jnp.arange(padded, dtype=jnp.int32) < count)[:, None]
    old = jnp.pad(momentum[0], ((0, padded - cap), (0, 0)))
    kept, nests = [], []
    for chunk in range(CHUNKS):
        for side in range(2):
            first = (chunk * 2 + side) * part
            _, terms = state[chunk, side]
            mean_grad = total(terms, [0])[0] / replicas
            buffer_new = momentum_rate * old[:, first : first + part] + mean_grad
            kept.append(jnp.where(live, buffer_new, 0.0)[:cap])
            nests.append(jnp.where(live, mean_grad + momentum_rate * buffer_new, 0.0).astype(bf16))
    kept_state = jnp.concatenate(kept, axis=1)

    held = []
    for chunk in range(CHUNKS):
        own = jnp.concatenate(nests[2 * chunk : 2 * chunk + 2], axis=1)
        held.append([own] + [to_owner(own, k) for k in range(groups - 1)])
    sums = [gram_call(parts) for parts in held[:-1]]
    factors = chain_call(width, sums, held[-1])
    is_owner = fsdp == (groups - 1) // 2 + (me & 1)
    rows = []
    for parts in held:
        own, *others = apply_call(factors, parts)
        back = [from_owner(other, k) for k, other in enumerate(others)]
        rows.append(jnp.where(is_owner, own, sum(back[1:], back[0]))[:cap])
    update = jnp.concatenate(rows, axis=1)
    return (kept_state[None], update[None])


def solution(mesh):
    placed = (P("rep", None, "fsdp", None), P("rep", "fsdp", None), P("rep", None))
    return jax.shard_map(
        functools.partial(per_device, mesh.shape["fsdp"], mesh.shape["rep"]),
        mesh=mesh,
        in_specs=placed,
        out_specs=(P("rep", "fsdp", None), P("rep", "fsdp", None)),
        check_vma=False,
    )
```

```python
import functools
import math

import jax
import jax.numpy as jnp
from jax import lax
from jax.experimental import pallas as pl
from jax.experimental.pallas import tpu as pltpu
from jax.sharding import PartitionSpec as P

ITERS = 3
FIRST_SHARE = 7 / 14

momentum_rate = 0.95
coef_a = 3.4445
coef_b = -4.775
coef_c = 2.0315

AXES = ("fsdp", "rep")
VMEM_LIMIT = 24 * 1024 * 1024
LANES = 128
TILE = 256
NEST_COST = 5_000_000
bf16 = jnp.bfloat16
f32 = jnp.float32


def dot(left, right):
    return jnp.dot(left, right, preferred_element_type=f32)


def two(value):
    high = value.astype(bf16)
    return high, (value - high.astype(f32)).astype(bf16)


def in_vmem(count):
    return [pl.BlockSpec(memory_space=pltpu.VMEM)] * count


def in_smem(count):
    return [pl.BlockSpec(memory_space=pltpu.SMEM)] * count


def call(body, outs, inputs, specs, after=(), scratch=(), hold=True, cost=1):
    count = len(inputs)

    def kernel(*refs):
        body(*refs[:count], *refs[count + len(after) :])

    return pl.pallas_call(
        kernel,
        out_shape=tuple(pltpu.VMEM(o.shape, o.dtype) if hold else o for o in outs),
        in_specs=list(specs) + [pl.BlockSpec(memory_space=pl.ANY)] * len(after),
        out_specs=tuple(in_vmem(len(outs))),
        scratch_shapes=list(scratch),
        compiler_params=pltpu.CompilerParams(vmem_limit_bytes=VMEM_LIMIT),
        cost_estimate=pl.CostEstimate(flops=1, bytes_accessed=cost, transcendentals=0),
    )(*inputs, *after)


def split(flat, mats, cap, padded, first, width, after):
    half = mats // 2
    rows = min(TILE // mats, cap)
    size = rows * mats
    blocks = -(-cap // rows)
    tiles = [(at, min(TILE, width - at)) for at in range(0, width, TILE)]

    def body(x_ref, keep_ref, send_ref, held_ref, sems):
        copies = [
            pltpu.make_async_copy(
                x_ref.at[:, first + at : first + at + wide], held_ref.at[:, at : at + wide], sems.at[i]
            )
            for i, (at, wide) in enumerate(tiles)
        ]
        for copy in copies:
            copy.start()
        me = lax.axis_index("rep")
        out_row = lax.broadcasted_iota(jnp.int32, (size, 1), 0)
        in_row = lax.broadcasted_iota(jnp.int32, (size, size), 1)
        place = out_row // rows
        within = out_row - place * rows
        j = jnp.where(place < half, 2 * place, 2 * (place - half) + 1)
        matrix = jnp.bitwise_xor(j, me)
        chosen = {}
        for block in range(blocks):
            start = min(block * rows, cap - rows)
            shift = block * rows - start
            if shift not in chosen:
                source = jnp.where(within < rows - shift, (within + shift) * mats + matrix, -1)
                chosen[shift] = jnp.where(in_row == source, 1.0, 0.0).astype(bf16)
        for copy, (at, wide) in zip(copies, tiles):
            copy.wait()
            for block in range(blocks):
                start = min(block * rows, cap - rows)
                moved = dot(
                    chosen[block * rows - start],
                    held_ref[start * mats : start * mats + size, at : at + wide],
                ).reshape(mats, rows, wide)
                here = min(rows, padded - block * rows)
                to = slice(block * rows, block * rows + here)
                keep_ref[:, to, at : at + wide] = moved[:half, :here].astype(bf16)
                send_ref[:, to, at : at + wide] = moved[half:, :here].astype(bf16)
        if blocks * rows < padded:
            rest = padded - blocks * rows
            keep_ref[:, blocks * rows :, :] = jnp.zeros((half, rest, width), bf16)
            send_ref[:, blocks * rows :, :] = jnp.zeros((half, rest, width), bf16)

    out = jax.ShapeDtypeStruct((half, padded, width), bf16)
    return call(
        body,
        [out, out],
        [pltpu.with_memory_space_constraint(flat, pltpu.HBM)],
        [pl.BlockSpec(memory_space=pltpu.HBM)],
        after,
        [pltpu.VMEM((flat.shape[0], width), bf16), pltpu.SemaphoreType.DMA((len(tiles),))],
    )


def fold(terms, plans, part, padded):
    def body(*refs):
        inputs, outs = refs[: len(terms)], refs[len(terms) :]
        for out, plan in zip(outs, plans):
            for row in range(0, padded, 16):
                to = slice(row, row + 16)
                for i, parts in enumerate(plan):
                    added = None
                    for term, place, at in parts:
                        value = inputs[term][place, to, at : at + part].astype(f32)
                        added = value if added is None else added + value
                    out[i, to, :] = added.astype(bf16)

    outs = [jax.ShapeDtypeStruct((len(plan), padded, part), bf16) for plan in plans]
    return call(body, outs, terms, in_vmem(len(terms)))


def linear_rows(ref, row, cap, blocks, block):
    here = max(0, min(8, cap - row))
    found = []
    if here:
        found.append(ref[pl.ds(row * blocks + block, here, stride=blocks), :])
    if here < 8:
        found.append(jnp.zeros((8 - here, LANES), f32))
    return found[0] if len(found) == 1 else jnp.concatenate(found, axis=0)


def live_count(offsets_ref):
    device = lax.axis_index("fsdp")
    return offsets_ref[0, device + 1] - offsets_ref[0, device]


def nesterov(offsets, linear, terms, plans, part, first, cap, padded, replicas, after):
    blocks = linear.shape[0] // cap
    width = part * len(plans)

    def body(*refs):
        offsets_ref, linear_ref, *inputs = refs[: 2 + len(terms)]
        out_ref, mean_ref = refs[2 + len(terms) :]
        count = live_count(offsets_ref)
        for row in range(0, padded, 16):
            slot = lax.broadcasted_iota(jnp.int32, (16, LANES), 0) + row
            to = slice(row, row + 16)
            for side, plan in enumerate(plans):
                for column in range(0, part, LANES):
                    added = None
                    for term, place, at in plan:
                        value = inputs[term][place, to, at + column : at + column + LANES].astype(f32)
                        added = value if added is None else added + value
                    mean = added * (1.0 / replicas)
                    here = side * part + column
                    block = (first + here) // LANES
                    old = jnp.concatenate(
                        [linear_rows(linear_ref, row + i, cap, blocks, block) for i in (0, 8)], axis=0
                    )
                    new = momentum_rate * old + mean
                    value = jnp.where(slot < count, mean + momentum_rate * new, 0.0)
                    out_ref[to, here : here + LANES] = value.astype(bf16)
                    mean_ref[to, here : here + LANES] = mean

    outs = [jax.ShapeDtypeStruct((padded, width), bf16), jax.ShapeDtypeStruct((padded, width), f32)]
    specs = in_smem(1) + in_vmem(1 + len(terms))
    return call(body, outs, [offsets, linear, *terms], specs, after, cost=NEST_COST)


def keep_state(offsets, linear, means, cap, after):
    blocks = linear.shape[0] // cap

    def body(offsets_ref, linear_ref, *refs):
        inputs, out_ref = refs[:-1], refs[-1]
        count = live_count(offsets_ref)
        for row in range(0, cap, 8):
            here = min(8, cap - row)
            slot = lax.broadcasted_iota(jnp.int32, (here, LANES), 0) + row
            first = 0
            for mean_ref in inputs:
                for column in range(0, mean_ref.shape[1], LANES):
                    at = pl.ds(row * blocks + (first + column) // LANES, here, stride=blocks)
                    new = momentum_rate * linear_ref[at, :] + mean_ref[
                        row : row + here, column : column + LANES
                    ]
                    out_ref[at, :] = jnp.where(slot < count, new, 0.0)
                first += mean_ref.shape[1]

    outs = [jax.ShapeDtypeStruct(linear.shape, f32)]
    specs = in_smem(1) + in_vmem(1 + len(means))
    return call(body, outs, [offsets, linear, *means], specs, after, hold=False)[0]


def gram_of(parts, stack_ref):
    rows = parts[0].shape[0]
    for i, part in enumerate(parts):
        stack_ref[i * rows : (i + 1) * rows, :] = part[...]
    return lax.dot_general(
        stack_ref[...], stack_ref[...], (((1,), (1,)), ((), ())), preferred_element_type=f32
    )


def gram(parts, after):
    size, width = len(parts) * parts[0].shape[0], parts[0].shape[1]

    def body(*refs):
        *inputs, stack_ref, out_ref = refs
        out_ref[...] = gram_of(inputs, stack_ref)

    outs = [jax.ShapeDtypeStruct((size, width), bf16), jax.ShapeDtypeStruct((size, size), f32)]
    return call(body, outs, parts, in_vmem(len(parts)), after)


def chain(full_width, sums, parts, after):
    groups = len(parts)
    rows, width = parts[0].shape
    size = groups * rows

    def body(*refs):
        earlier, inputs = refs[: len(sums)], refs[len(sums) : -3]
        stack_ref, factor_ref, alpha_ref = refs[-3:]
        gram = gram_of(inputs, stack_ref)
        for earlier_ref in earlier:
            gram = gram + earlier_ref[...]
        diagonal = lax.broadcasted_iota(jnp.int32, (size, size), 0) == lax.broadcasted_iota(
            jnp.int32, (size, size), 1
        )
        trace = jnp.sum(jnp.where(diagonal, gram, 0.0), keepdims=True)
        scale = 1.0 / (jnp.sqrt(trace) + 1e-07)
        gram = (gram * scale) * scale
        rest = None
        power = 1.0
        for iteration in range(ITERS):
            rounded = gram.astype(bf16)
            square = dot(rounded, rounded)
            poly = (coef_b * rounded.astype(f32) + coef_c * square).astype(bf16)
            if rest is None:
                rest = poly.astype(f32)
            else:
                rest_high, rest_low = two(rest)
                rest = (
                    coef_a * rest
                    + power * poly.astype(f32)
                    + (dot(poly, rest_high) + dot(poly, rest_low))
                )
            power = power * coef_a
            if iteration < ITERS - 1:
                gram_high, gram_low = two(gram)
                left = coef_a * gram + (dot(poly, gram_high) + dot(poly, gram_low))
                left_high, left_low = two(left)
                gram = coef_a * left + (dot(left_high, poly) + dot(left_low, poly))
        scale = scale * math.sqrt(full_width)
        high, low = two(rest * scale)
        for i in range(groups):
            factor_ref[i, :rows, :] = high[i * rows : (i + 1) * rows]
            factor_ref[i, rows:, :] = low[i * rows : (i + 1) * rows]
        alpha_ref[...] = jnp.broadcast_to(scale * power, alpha_ref.shape)

    outs = [
        jax.ShapeDtypeStruct((size, width), bf16),
        jax.ShapeDtypeStruct((groups, 2 * rows, size), bf16),
        jax.ShapeDtypeStruct((8, LANES), f32),
    ]
    return call(body, outs, [*sums, *parts], in_vmem(len(sums) + groups), after)


def apply_rows(index, factor_ref, alpha_ref, stacks, out_ref):
    rows = factor_ref.shape[1] // 2
    height = out_ref.shape[0]
    left = factor_ref[index]
    own = slice(index * rows, (index + 1) * rows)
    first = 0
    for stack_ref in stacks:
        for at in range(0, stack_ref.shape[1], TILE):
            to = slice(at, min(at + TILE, stack_ref.shape[1]))
            both = dot(left, stack_ref[:, to])
            result = both[:rows] + both[rows:] + alpha_ref[0:1, 0:1] * stack_ref[own, to].astype(f32)
            out_ref[:, first + to.start : first + to.stop] = result[:height].astype(bf16)
        first += stack_ref.shape[1]


def rows_of(factor, alpha, stacks, index, after):
    def body(factor_ref, alpha_ref, *refs):
        apply_rows(index, factor_ref, alpha_ref, refs[:-1], refs[-1])

    outs = [jax.ShapeDtypeStruct((factor.shape[1] // 2, sum(s.shape[1] for s in stacks)), bf16)]
    return call(body, outs, [factor, alpha, *stacks], in_vmem(2 + len(stacks)), after)[0]


def own_or_received(owners, factor, alpha, stacks, received, cap):
    def body(factor_ref, alpha_ref, *refs):
        *inputs, out_ref = refs
        mine = lax.axis_index("fsdp") == owners + lax.rem(lax.axis_index("rep"), 2)

        @pl.when(mine)
        def _():
            apply_rows(0, factor_ref, alpha_ref, inputs[: len(stacks)], out_ref)

        @pl.when(jnp.logical_not(mine))
        def _():
            for row in range(0, cap, 16):
                to = slice(row, min(row + 16, cap))
                added = None
                for came in inputs[len(stacks) :]:
                    value = came[to, :]
                    added = value if added is None else added + value
                out_ref[to, :] = added

    outs = [jax.ShapeDtypeStruct((cap, received[0].shape[1]), bf16)]
    specs = in_vmem(2 + len(stacks) + len(received))
    return call(body, outs, [factor, alpha, *stacks, *received], specs, hold=False)[0]


def per_device(groups, replicas, gradients, momentum, offsets):
    _, mats, cap, width = gradients.shape
    padded = -(-cap // 16) * 16
    bits = [1 << i for i in range(replicas.bit_length() - 1)]

    def swap(value, bit):
        pairs = [(f * replicas + r, f * replicas + (r ^ bit)) for f in range(groups) for r in range(replicas)]
        return lax.ppermute(value, AXES, pairs)

    def owner(r):
        return (groups - 1) // 2 + r % 2

    def others(r):
        return sorted((f for f in range(groups) if f != owner(r)), key=lambda f: -abs(f - owner(r)))

    def to_owner(value, k):
        pairs = [(others(r)[k] * replicas + r, owner(r) * replicas + r) for r in range(replicas)]
        return lax.ppermute(value, AXES, pairs)

    def from_owner(value, k):
        pairs = [(owner(r) * replicas + r, others(r)[k] * replicas + r) for r in range(replicas)]
        return lax.ppermute(value, AXES, pairs)

    flat = jnp.transpose(gradients[0], (1, 0, 2)).reshape(cap * mats, width)
    linear = momentum[0].reshape(cap * (width // LANES), LANES)

    unit = 2 * LANES
    head = max(1, round(width // unit * FIRST_SHARE)) * unit
    chunks = [(0, head), (head, width - head)]
    orders = [bits[1:], bits[1:][::-1]]
    terms, plans = [], []
    last = ()
    for first, wide in chunks:
        keep, send = split(flat, mats, cap, padded, first, wide, last)
        last = (keep,)
        terms.append([keep, swap(send, bits[0])])
        plans.append(
            [{2 * i: [(t, i, side * (wide // 2)) for t in range(2)] for i in range(mats // 2)} for side in range(2)]
        )
    for level in range(len(bits) - 1):
        for chunk, (_, wide) in enumerate(chunks):
            moving = [[j for j in plan if j & order[level]] for plan, order in zip(plans[chunk], orders)]
            wanted = [[plan[j] for j in away] for plan, away in zip(plans[chunk], moving)]
            sends = fold(terms[chunk], wanted, wide // 2, padded)
            last = (sends[0],)
            for side, away in enumerate(moving):
                bit = orders[side][level]
                terms[chunk].append(swap(sends[side], bit))
                for place, j in enumerate(away):
                    plans[chunk][side][j ^ bit].append((len(terms[chunk]) - 1, place, 0))
                    del plans[chunk][side][j]

    means, held = [], []
    for chunk, (first, wide) in enumerate(chunks):
        sources = [plan[0] for plan in plans[chunk]]
        own, mean = nesterov(
            offsets, linear, terms[chunk], sources, wide // 2, first, cap, padded, replicas, last
        )
        last = (own,)
        means.append(mean)
        held.append([own] + [to_owner(own, k) for k in range(groups - 1)])
    kept_state = keep_state(offsets, linear, means, cap, last)
    stacks, sums = [], []
    for parts in held[:-1]:
        stack, partial = gram(parts, (kept_state,))
        stacks.append(stack)
        sums.append(partial)
    stack, factor, alpha = chain(width, sums, held[-1], ())
    stacks.append(stack)
    back = []
    last = ()
    for k in range(groups - 1):
        result = rows_of(factor, alpha, stacks, k + 1, last)
        last = (result,)
        back.append(from_owner(result, k))
    update = own_or_received((groups - 1) // 2, factor, alpha, stacks, back, cap)
    return (kept_state.reshape(1, cap, width), update[None])


def solution(mesh):
    placed = (P("rep", None, "fsdp", None), P("rep", "fsdp", None), P("rep", None))
    return jax.shard_map(
        functools.partial(per_device, mesh.shape["fsdp"], mesh.shape["rep"]),
        mesh=mesh,
        in_specs=placed,
        out_specs=(P("rep", "fsdp", None), P("rep", "fsdp", None)),
        check_vma=False,
    )
```

```python
import functools
import math

import jax
import jax.numpy as jnp
from jax import lax
from jax.experimental import pallas as pl
from jax.experimental.pallas import tpu as pltpu
from jax.sharding import PartitionSpec as P

ITERS = 3
SHARES = (7, 7)
STEPS = (('S', 0), ('S', 1), ('H', 0, 0), ('H', 1, 0), ('H', 0, 1), ('H', 1, 1), ('N', 0), ('N', 1))

momentum_rate = 0.95
coef_a = 3.4445
coef_b = -4.775
coef_c = 2.0315

AXES = ("fsdp", "rep")
VMEM_LIMIT = 24 * 1024 * 1024
LANES = 128
TILE = 256
BESIDE = {'gate0': 1, 'gate1': 1, 'nest0': 8.7, 'nest1792': 8.7}
bf16 = jnp.bfloat16
f32 = jnp.float32


def dot(left, right):
    return jnp.dot(left, right, preferred_element_type=f32)


def two(value):
    high = value.astype(bf16)
    return high, (value - high.astype(f32)).astype(bf16)


def in_vmem(count):
    return [pl.BlockSpec(memory_space=pltpu.VMEM)] * count


def in_smem(count):
    return [pl.BlockSpec(memory_space=pltpu.SMEM)] * count


def call(body, outs, inputs, specs, after=(), scratch=(), hold=True, name="step"):
    count = len(inputs)

    def kernel(*refs):
        body(*refs[:count], *refs[count + len(after) :])

    return pl.pallas_call(
        kernel,
        out_shape=tuple(pltpu.VMEM(o.shape, o.dtype) if hold else o for o in outs),
        in_specs=list(specs) + [pl.BlockSpec(memory_space=pl.ANY)] * len(after),
        out_specs=tuple(in_vmem(len(outs))),
        scratch_shapes=list(scratch),
        name=name,
        compiler_params=pltpu.CompilerParams(vmem_limit_bytes=VMEM_LIMIT),
        cost_estimate=pl.CostEstimate(flops=max(1, int(BESIDE.get(name, 0) * 1.15e9)), bytes_accessed=1, transcendentals=0),
    )(*inputs, *after)


def split(flat, mats, cap, padded, first, width, after):
    half = mats // 2
    rows = min(TILE // mats, cap)
    size = rows * mats
    blocks = -(-cap // rows)
    starts = [min(block * rows, cap - rows) for block in range(blocks)]

    def body(x_ref, keep_ref, send_ref, held_ref, sems):
        copies = [
            pltpu.make_async_copy(
                x_ref.at[start * mats : start * mats + size, first : first + width], held_ref.at[i], sems.at[i]
            )
            for i, start in enumerate(starts)
        ]
        for copy in copies:
            copy.start()
        me = lax.axis_index("rep")
        out_row = lax.broadcasted_iota(jnp.int32, (size, 1), 0)
        in_row = lax.broadcasted_iota(jnp.int32, (size, size), 1)
        place = out_row // rows
        within = out_row - place * rows
        j = jnp.where(place < half, 2 * place, 2 * (place - half) + 1)
        matrix = jnp.bitwise_xor(j, me)
        chosen = {}
        for block, start in enumerate(starts):
            shift = block * rows - start
            if shift not in chosen:
                source = jnp.where(within < rows - shift, (within + shift) * mats + matrix, -1)
                chosen[shift] = jnp.where(in_row == source, 1.0, 0.0).astype(bf16)
        for block, start in enumerate(starts):
            copies[block].wait()
            for at in range(0, width, TILE):
                wide = min(TILE, width - at)
                moved = dot(chosen[block * rows - start], held_ref[block, :, at : at + wide])
                moved = moved.reshape(mats, rows, wide)
                here = min(rows, padded - block * rows)
                to = slice(block * rows, block * rows + here)
                keep_ref[:, to, at : at + wide] = moved[:half, :here].astype(bf16)
                send_ref[:, to, at : at + wide] = moved[half:, :here].astype(bf16)
        if blocks * rows < padded:
            rest = padded - blocks * rows
            keep_ref[:, blocks * rows :, :] = jnp.zeros((half, rest, width), bf16)
            send_ref[:, blocks * rows :, :] = jnp.zeros((half, rest, width), bf16)

    out = jax.ShapeDtypeStruct((half, padded, width), bf16)
    return call(
        body,
        [out, out],
        [pltpu.with_memory_space_constraint(flat, pltpu.HBM)],
        [pl.BlockSpec(memory_space=pltpu.HBM)],
        after,
        [pltpu.VMEM((blocks, size, width), bf16), pltpu.SemaphoreType.DMA((blocks,))],
        name=f"split{first}",
    )


def added(inputs, parts, rows, width):
    total = None
    for term, place, at in parts:
        value = inputs[term][place, rows, at : at + width].astype(f32)
        total = value if total is None else total + value
    return total


def fold(terms, plans, padded, after, name):
    def body(*refs):
        inputs, outs = refs[: len(terms)], refs[len(terms) :]
        for out, plan in zip(outs, plans):
            for row in range(0, padded, 16):
                to = slice(row, row + 16)
                for i, segments in enumerate(plan):
                    at = 0
                    for width, parts in segments:
                        out[i, to, at : at + width] = added(inputs, parts, to, width).astype(bf16)
                        at += width

    outs = [jax.ShapeDtypeStruct((len(plan), padded, sum(w for w, _ in plan[0])), bf16) for plan in plans]
    return call(body, outs, terms, in_vmem(len(terms)), after, name=name)


def linear_rows(ref, row, cap, blocks, block):
    here = max(0, min(8, cap - row))
    found = []
    if here:
        found.append(ref[pl.ds(row * blocks + block, here, stride=blocks), :])
    if here < 8:
        found.append(jnp.zeros((8 - here, LANES), f32))
    return found[0] if len(found) == 1 else jnp.concatenate(found, axis=0)


def live_count(offsets_ref):
    device = lax.axis_index("fsdp")
    return offsets_ref[0, device + 1] - offsets_ref[0, device]


def nesterov(offsets, linear, terms, segments, first, wide, cap, padded, replicas, after):
    blocks = linear.shape[0] // cap

    def body(*refs):
        offsets_ref, linear_ref, *inputs = refs[: 2 + len(terms)]
        out_ref, mean_ref = refs[2 + len(terms) :]
        count = live_count(offsets_ref)
        for row in range(0, padded, 16):
            slot = lax.broadcasted_iota(jnp.int32, (16, LANES), 0) + row
            to = slice(row, row + 16)
            for start, width, parts in segments:
                for column in range(0, width, LANES):
                    here = [(term, place, at + column) for term, place, at in parts]
                    mean = added(inputs, here, to, LANES) * (1.0 / replicas)
                    block = (start + column) // LANES
                    old = jnp.concatenate(
                        [linear_rows(linear_ref, row + i, cap, blocks, block) for i in (0, 8)], axis=0
                    )
                    new = momentum_rate * old + mean
                    value = jnp.where(slot < count, mean + momentum_rate * new, 0.0)
                    at = start + column - first
                    out_ref[to, at : at + LANES] = value.astype(bf16)
                    mean_ref[to, at : at + LANES] = mean

    outs = [jax.ShapeDtypeStruct((padded, wide), bf16), jax.ShapeDtypeStruct((padded, wide), f32)]
    specs = in_smem(1) + in_vmem(1 + len(terms))
    return call(body, outs, [offsets, linear, *terms], specs, after, name=f"nest{first}")


def keep_state(offsets, linear, means, cap, after):
    blocks = linear.shape[0] // cap

    def body(offsets_ref, linear_ref, *refs):
        inputs, out_ref = refs[:-1], refs[-1]
        count = live_count(offsets_ref)
        for row in range(0, cap, 8):
            here = min(8, cap - row)
            slot = lax.broadcasted_iota(jnp.int32, (here, LANES), 0) + row
            first = 0
            for mean_ref in inputs:
                for column in range(0, mean_ref.shape[1], LANES):
                    at = pl.ds(row * blocks + (first + column) // LANES, here, stride=blocks)
                    new = momentum_rate * linear_ref[at, :] + mean_ref[
                        row : row + here, column : column + LANES
                    ]
                    out_ref[at, :] = jnp.where(slot < count, new, 0.0)
                first += mean_ref.shape[1]

    outs = [jax.ShapeDtypeStruct(linear.shape, f32)]
    specs = in_smem(1) + in_vmem(1 + len(means))
    return call(body, outs, [offsets, linear, *means], specs, after, hold=False, name="keep")[0]


def gram_of(parts, stack_ref):
    rows = parts[0].shape[0]
    for i, part in enumerate(parts):
        stack_ref[i * rows : (i + 1) * rows, :] = part[...]
    return lax.dot_general(
        stack_ref[...], stack_ref[...], (((1,), (1,)), ((), ())), preferred_element_type=f32
    )


def gram(parts, after, name):
    size, width = len(parts) * parts[0].shape[0], parts[0].shape[1]

    def body(*refs):
        *inputs, stack_ref, out_ref = refs
        out_ref[...] = gram_of(inputs, stack_ref)

    outs = [jax.ShapeDtypeStruct((size, width), bf16), jax.ShapeDtypeStruct((size, size), f32)]
    return call(body, outs, parts, in_vmem(len(parts)), after, name=name)


def chain(full_width, sums, parts, after):
    groups = len(parts)
    rows, width = parts[0].shape
    size = groups * rows

    def body(*refs):
        earlier, inputs = refs[: len(sums)], refs[len(sums) : -3]
        stack_ref, factor_ref, alpha_ref = refs[-3:]
        gram = gram_of(inputs, stack_ref)
        for earlier_ref in earlier:
            gram = gram + earlier_ref[...]
        diagonal = lax.broadcasted_iota(jnp.int32, (size, size), 0) == lax.broadcasted_iota(
            jnp.int32, (size, size), 1
        )
        trace = jnp.sum(jnp.where(diagonal, gram, 0.0), keepdims=True)
        scale = 1.0 / (jnp.sqrt(trace) + 1e-07)
        gram = (gram * scale) * scale
        rest = None
        power = 1.0
        for iteration in range(ITERS):
            rounded = gram.astype(bf16)
            square = dot(rounded, rounded)
            poly = (coef_b * rounded.astype(f32) + coef_c * square).astype(bf16)
            if rest is None:
                rest = poly.astype(f32)
            else:
                rest_high, rest_low = two(rest)
                rest = (
                    coef_a * rest
                    + power * poly.astype(f32)
                    + (dot(poly, rest_high) + dot(poly, rest_low))
                )
            power = power * coef_a
            if iteration < ITERS - 1:
                gram_high, gram_low = two(gram)
                left = coef_a * gram + (dot(poly, gram_high) + dot(poly, gram_low))
                left_high, left_low = two(left)
                gram = coef_a * left + (dot(left_high, poly) + dot(left_low, poly))
        scale = scale * math.sqrt(full_width)
        high, low = two(rest * scale)
        for i in range(groups):
            factor_ref[i, :rows, :] = high[i * rows : (i + 1) * rows]
            factor_ref[i, rows:, :] = low[i * rows : (i + 1) * rows]
        alpha_ref[...] = jnp.broadcast_to(scale * power, alpha_ref.shape)

    outs = [
        jax.ShapeDtypeStruct((size, width), bf16),
        jax.ShapeDtypeStruct((groups, 2 * rows, size), bf16),
        jax.ShapeDtypeStruct((8, LANES), f32),
    ]
    return call(body, outs, [*sums, *parts], in_vmem(len(sums) + groups), after, name="chain")


def apply_rows(index, factor_ref, alpha_ref, stacks, out_ref):
    rows = factor_ref.shape[1] // 2
    height = out_ref.shape[0]
    left = factor_ref[index]
    own = slice(index * rows, (index + 1) * rows)
    first = 0
    for stack_ref in stacks:
        for at in range(0, stack_ref.shape[1], TILE):
            to = slice(at, min(at + TILE, stack_ref.shape[1]))
            both = dot(left, stack_ref[:, to])
            result = both[:rows] + both[rows:] + alpha_ref[0:1, 0:1] * stack_ref[own, to].astype(f32)
            out_ref[:, first + to.start : first + to.stop] = result[:height].astype(bf16)
        first += stack_ref.shape[1]


def rows_of(factor, alpha, stacks, index, after):
    def body(factor_ref, alpha_ref, *refs):
        apply_rows(index, factor_ref, alpha_ref, refs[:-1], refs[-1])

    outs = [jax.ShapeDtypeStruct((factor.shape[1] // 2, sum(s.shape[1] for s in stacks)), bf16)]
    return call(body, outs, [factor, alpha, *stacks], in_vmem(2 + len(stacks)), after, name=f"rows{index}")[0]


def gate(after, name):
    def body(out_ref):
        out_ref[...] = jnp.zeros_like(out_ref)

    return call(body, [jax.ShapeDtypeStruct((8, LANES), f32)], [], [], after, name=name)[0]


def own_or_received(owners, factor, alpha, stacks, received, cap, after):
    def body(factor_ref, alpha_ref, *refs):
        *inputs, out_ref = refs
        mine = lax.axis_index("fsdp") == owners + lax.rem(lax.axis_index("rep"), 2)

        @pl.when(mine)
        def _():
            apply_rows(0, factor_ref, alpha_ref, inputs[: len(stacks)], out_ref)

        @pl.when(jnp.logical_not(mine))
        def _():
            for row in range(0, cap, 16):
                to = slice(row, min(row + 16, cap))
                added = None
                for came in inputs[len(stacks) :]:
                    value = came[to, :]
                    added = value if added is None else added + value
                out_ref[to, :] = added

    outs = [jax.ShapeDtypeStruct((cap, received[0].shape[1]), bf16)]
    specs = in_vmem(2 + len(stacks) + len(received))
    return call(body, outs, [factor, alpha, *stacks, *received], specs, after, hold=False, name="last")[0]


def per_device(groups, replicas, gradients, momentum, offsets):
    _, mats, cap, width = gradients.shape
    padded = -(-cap // 16) * 16
    bits = [1 << i for i in range(replicas.bit_length() - 1)]

    def swap(value, bit):
        pairs = [(f * replicas + r, f * replicas + (r ^ bit)) for f in range(groups) for r in range(replicas)]
        return lax.ppermute(value, AXES, pairs)

    def owner(r):
        return (groups - 1) // 2 + r % 2

    def others(r):
        return sorted((f for f in range(groups) if f != owner(r)), key=lambda f: -abs(f - owner(r)))

    def to_owner(value, k):
        pairs = [(others(r)[k] * replicas + r, owner(r) * replicas + r) for r in range(replicas)]
        return lax.ppermute(value, AXES, pairs)

    def from_owner(value, k):
        pairs = [(owner(r) * replicas + r, others(r)[k] * replicas + r) for r in range(replicas)]
        return lax.ppermute(value, AXES, pairs)

    flat = jnp.transpose(gradients[0], (1, 0, 2)).reshape(cap * mats, width)
    linear = momentum[0].reshape(cap * (width // LANES), LANES)

    chunks, first = [], 0
    for share in SHARES:
        wide = width // sum(SHARES) * share
        chunks.append((first, wide))
        first += wide
    orders = [bits[1:], bits[1:][::-1]]
    last = ()

    def split_piece(first, wide):
        nonlocal last
        keep, send = split(flat, mats, cap, padded, first, wide, last)
        last = (keep,)
        half = wide // 2
        plans = [
            {2 * i: [(first + side * half, half, [(t, i, side * half) for t in range(2)])] for i in range(mats // 2)}
            for side in range(2)
        ]
        return [keep, swap(send, bits[0])], plans

    def halve(level, terms, plans):
        nonlocal last
        moving = [[j for j in plan if j & order[level]] for plan, order in zip(plans, orders)]
        wanted = [[[(w, parts) for _, w, parts in plan[j]] for j in away] for plan, away in zip(plans, moving)]
        name = f"fold{level}_{plans[0][0][0][0]}"
        sends = fold(terms, wanted, padded, last, name)
        last = (sends[0],)
        for side, away in enumerate(moving):
            bit = orders[side][level]
            terms.append(swap(sends[side], bit))
            for place, j in enumerate(away):
                at = 0
                for _, segment, parts in plans[side][j ^ bit]:
                    parts.append((len(terms) - 1, place, at))
                    at += segment
                del plans[side][j]

    means, held = [], []

    def finish(chunk, terms, plans):
        nonlocal last
        segments = [segment for plan in plans for segment in plan[0]]
        own, mean = nesterov(offsets, linear, terms, segments, *chunk, cap, padded, replicas, last)
        last = (own,)
        means.append(mean)
        held.append([own] + [to_owner(own, k) for k in range(groups - 1)])

    levels = len(bits) - 1
    work, arrived, reached = {}, {}, [0] * len(chunks)

    def halve_next(chunk):
        level = reached[chunk]
        halve(level, *work[chunk])
        arrived[chunk, level] = tuple(work[chunk][0][-2:])
        reached[chunk] += 1

    for kind, chunk, *more in STEPS:
        if more and isinstance(more[-1], tuple):
            last += arrived.get(more[-1], ())
        if kind == "S":
            work[chunk] = split_piece(*chunks[chunk])
        elif kind == "H" and more[0] < levels:
            halve_next(chunk)
        elif kind == "N":
            while reached[chunk] < levels:
                halve_next(chunk)
            finish(chunks[chunk], *work[chunk])
    kept_state = keep_state(offsets, linear, means, cap, last)
    kept_there = pltpu.with_memory_space_constraint(kept_state, pltpu.HBM)
    stacks, sums = [], []
    for parts in held[:-1]:
        stack, partial = gram(parts, (kept_there,), f"gram{len(sums)}")
        stacks.append(stack)
        sums.append(partial)
    stack, factor, alpha = chain(width, sums, held[-1], ())
    stacks.append(stack)
    back = []
    last = ()
    for k in range(groups - 1):
        result = rows_of(factor, alpha, stacks, k + 1, last)
        last = (result,)
        back.append(from_owner(result, k))
    last = ()
    for k, came in enumerate(back[:-1]):
        last = (gate((came, *last), f"gate{k}"),)
    update = own_or_received((groups - 1) // 2, factor, alpha, stacks, back, cap, last)
    return (kept_state.reshape(1, cap, width), update[None])


def solution(mesh):
    placed = (P("rep", None, "fsdp", None), P("rep", "fsdp", None), P("rep", None))
    return jax.shard_map(
        functools.partial(per_device, mesh.shape["fsdp"], mesh.shape["rep"]),
        mesh=mesh,
        in_specs=placed,
        out_specs=(P("rep", "fsdp", None), P("rep", "fsdp", None)),
        check_vma=False,
    )
```

```python
import functools
import math

import jax
import jax.numpy as jnp
from jax import lax
from jax.experimental import pallas as pl
from jax.experimental.pallas import tpu as pltpu
from jax.sharding import PartitionSpec as P

ITERS = 3
SHARES = (8, 6)
STEPS = (('S', 0), ('S', 1), ('H', 0, 0), ('H', 0, 1), ('H', 1, 0), ('N', 0), ('H', 1, 1), ('N', 1))

momentum_rate = 0.95
coef_a = 3.4445
coef_b = -4.775
coef_c = 2.0315

AXES = ("fsdp", "rep")
VMEM_LIMIT = 24 * 1024 * 1024
LANES = 128
TILE = 256
BESIDE = {'gate1': 1, 'nest0': 16, 'gram0': 0.5, 'fold1_0': 4, 'split2048': 1, 'gate0': 1}
bf16 = jnp.bfloat16
f32 = jnp.float32


def dot(left, right):
    return jnp.dot(left, right, preferred_element_type=f32)


def two(value):
    high = value.astype(bf16)
    return high, (value - high.astype(f32)).astype(bf16)


def in_vmem(count):
    return [pl.BlockSpec(memory_space=pltpu.VMEM)] * count


def in_smem(count):
    return [pl.BlockSpec(memory_space=pltpu.SMEM)] * count


def call(body, outs, inputs, specs, after=(), scratch=(), hold=True, name="step"):
    count = len(inputs)

    def kernel(*refs):
        body(*refs[:count], *refs[count + len(after) :])

    return pl.pallas_call(
        kernel,
        out_shape=tuple(pltpu.VMEM(o.shape, o.dtype) if hold else o for o in outs),
        in_specs=list(specs) + [pl.BlockSpec(memory_space=pl.ANY)] * len(after),
        out_specs=tuple(in_vmem(len(outs))),
        scratch_shapes=list(scratch),
        name=name,
        compiler_params=pltpu.CompilerParams(vmem_limit_bytes=VMEM_LIMIT),
        cost_estimate=pl.CostEstimate(flops=max(1, int(BESIDE.get(name, 0) * 1.15e9)), bytes_accessed=1, transcendentals=0),
    )(*inputs, *after)


def split(flat, mats, cap, padded, first, width, after):
    half = mats // 2
    rows = min(TILE // mats, cap)
    size = rows * mats
    blocks = -(-cap // rows)
    starts = [min(block * rows, cap - rows) for block in range(blocks)]

    def body(x_ref, keep_ref, send_ref, held_ref, sems):
        copies = [
            pltpu.make_async_copy(
                x_ref.at[start * mats : start * mats + size, first : first + width], held_ref.at[i], sems.at[i]
            )
            for i, start in enumerate(starts)
        ]
        for copy in copies:
            copy.start()
        me = lax.axis_index("rep")
        out_row = lax.broadcasted_iota(jnp.int32, (size, 1), 0)
        in_row = lax.broadcasted_iota(jnp.int32, (size, size), 1)
        place = out_row // rows
        within = out_row - place * rows
        j = jnp.where(place < half, 2 * place, 2 * (place - half) + 1)
        matrix = jnp.bitwise_xor(j, me)
        chosen = {}
        for block, start in enumerate(starts):
            shift = block * rows - start
            if shift not in chosen:
                source = jnp.where(within < rows - shift, (within + shift) * mats + matrix, -1)
                chosen[shift] = jnp.where(in_row == source, 1.0, 0.0).astype(bf16)
        for block, start in enumerate(starts):
            copies[block].wait()
            for at in range(0, width, TILE):
                wide = min(TILE, width - at)
                moved = dot(chosen[block * rows - start], held_ref[block, :, at : at + wide])
                moved = moved.reshape(mats, rows, wide)
                here = min(rows, padded - block * rows)
                to = slice(block * rows, block * rows + here)
                keep_ref[:, to, at : at + wide] = moved[:half, :here].astype(bf16)
                send_ref[:, to, at : at + wide] = moved[half:, :here].astype(bf16)
        if blocks * rows < padded:
            rest = padded - blocks * rows
            keep_ref[:, blocks * rows :, :] = jnp.zeros((half, rest, width), bf16)
            send_ref[:, blocks * rows :, :] = jnp.zeros((half, rest, width), bf16)

    out = jax.ShapeDtypeStruct((half, padded, width), bf16)
    return call(
        body,
        [out, out],
        [pltpu.with_memory_space_constraint(flat, pltpu.HBM)],
        [pl.BlockSpec(memory_space=pltpu.HBM)],
        after,
        [pltpu.VMEM((blocks, size, width), bf16), pltpu.SemaphoreType.DMA((blocks,))],
        name=f"split{first}",
    )


def added(inputs, parts, rows, width):
    total = None
    for term, place, at in parts:
        value = inputs[term][place, rows, at : at + width].astype(f32)
        total = value if total is None else total + value
    return total


def fold(terms, plans, padded, after, name):
    def body(*refs):
        inputs, outs = refs[: len(terms)], refs[len(terms) :]
        for out, plan in zip(outs, plans):
            for row in range(0, padded, 16):
                to = slice(row, row + 16)
                for i, segments in enumerate(plan):
                    at = 0
                    for width, parts in segments:
                        out[i, to, at : at + width] = added(inputs, parts, to, width).astype(bf16)
                        at += width

    outs = [jax.ShapeDtypeStruct((len(plan), padded, sum(w for w, _ in plan[0])), bf16) for plan in plans]
    return call(body, outs, terms, in_vmem(len(terms)), after, name=name)


def linear_rows(ref, row, cap, blocks, block):
    here = max(0, min(8, cap - row))
    found = []
    if here:
        found.append(ref[pl.ds(row * blocks + block, here, stride=blocks), :])
    if here < 8:
        found.append(jnp.zeros((8 - here, LANES), f32))
    return found[0] if len(found) == 1 else jnp.concatenate(found, axis=0)


def live_count(offsets_ref):
    device = lax.axis_index("fsdp")
    return offsets_ref[0, device + 1] - offsets_ref[0, device]


def nesterov(offsets, linear, terms, segments, first, wide, cap, padded, replicas, after):
    blocks = linear.shape[0] // cap

    def body(*refs):
        offsets_ref, linear_ref, *inputs = refs[: 2 + len(terms)]
        out_ref, mean_ref = refs[2 + len(terms) :]
        count = live_count(offsets_ref)
        for row in range(0, padded, 16):
            slot = lax.broadcasted_iota(jnp.int32, (16, LANES), 0) + row
            to = slice(row, row + 16)
            for start, width, parts in segments:
                for column in range(0, width, LANES):
                    here = [(term, place, at + column) for term, place, at in parts]
                    mean = added(inputs, here, to, LANES) * (1.0 / replicas)
                    block = (start + column) // LANES
                    old = jnp.concatenate(
                        [linear_rows(linear_ref, row + i, cap, blocks, block) for i in (0, 8)], axis=0
                    )
                    new = momentum_rate * old + mean
                    value = jnp.where(slot < count, mean + momentum_rate * new, 0.0)
                    at = start + column - first
                    out_ref[to, at : at + LANES] = value.astype(bf16)
                    mean_ref[to, at : at + LANES] = mean

    outs = [jax.ShapeDtypeStruct((padded, wide), bf16), jax.ShapeDtypeStruct((padded, wide), f32)]
    specs = in_smem(1) + in_vmem(1 + len(terms))
    return call(body, outs, [offsets, linear, *terms], specs, after, name=f"nest{first}")


def keep_state(offsets, linear, means, cap, after):
    blocks = linear.shape[0] // cap

    def body(offsets_ref, linear_ref, *refs):
        inputs, out_ref = refs[:-1], refs[-1]
        count = live_count(offsets_ref)
        for row in range(0, cap, 8):
            here = min(8, cap - row)
            slot = lax.broadcasted_iota(jnp.int32, (here, LANES), 0) + row
            first = 0
            for mean_ref in inputs:
                for column in range(0, mean_ref.shape[1], LANES):
                    at = pl.ds(row * blocks + (first + column) // LANES, here, stride=blocks)
                    new = momentum_rate * linear_ref[at, :] + mean_ref[
                        row : row + here, column : column + LANES
                    ]
                    out_ref[at, :] = jnp.where(slot < count, new, 0.0)
                first += mean_ref.shape[1]

    outs = [jax.ShapeDtypeStruct(linear.shape, f32)]
    specs = in_smem(1) + in_vmem(1 + len(means))
    return call(body, outs, [offsets, linear, *means], specs, after, hold=False, name="keep")[0]


def symmetric(block, size):
    if size <= TILE or size % LANES:
        return block(slice(0, size), slice(0, size))
    left = block(slice(0, size), slice(0, TILE))
    corner = block(slice(TILE, size), slice(TILE, size))
    top = jnp.concatenate([left[:TILE], left[TILE:].T], axis=1)
    return jnp.concatenate([top, jnp.concatenate([left[TILE:], corner], axis=1)], axis=0)


def gram_of(parts, stack_ref):
    rows = parts[0].shape[0]
    for i, part in enumerate(parts):
        stack_ref[i * rows : (i + 1) * rows, :] = part[...]

    def block(down, across):
        return lax.dot_general(
            stack_ref[down, :], stack_ref[across, :], (((1,), (1,)), ((), ())), preferred_element_type=f32
        )

    return symmetric(block, len(parts) * rows)


def gram(parts, after, name):
    size, width = len(parts) * parts[0].shape[0], parts[0].shape[1]

    def body(*refs):
        *inputs, stack_ref, out_ref = refs
        out_ref[...] = gram_of(inputs, stack_ref)

    outs = [jax.ShapeDtypeStruct((size, width), bf16), jax.ShapeDtypeStruct((size, size), f32)]
    return call(body, outs, parts, in_vmem(len(parts)), after, name=name)


def chain(full_width, sums, parts, after):
    groups = len(parts)
    rows, width = parts[0].shape
    size = groups * rows

    def body(*refs):
        earlier, inputs = refs[: len(sums)], refs[len(sums) : -3]
        stack_ref, factor_ref, alpha_ref = refs[-3:]
        gram = gram_of(inputs, stack_ref)
        for earlier_ref in earlier:
            gram = gram + earlier_ref[...]
        diagonal = lax.broadcasted_iota(jnp.int32, (size, size), 0) == lax.broadcasted_iota(
            jnp.int32, (size, size), 1
        )
        trace = jnp.sum(jnp.where(diagonal, gram, 0.0), keepdims=True)
        scale = 1.0 / (jnp.sqrt(trace) + 1e-07)
        gram = (gram * scale) * scale
        rest = None
        power = 1.0
        for iteration in range(ITERS):
            rounded = gram.astype(bf16)
            square = symmetric(lambda down, across: dot(rounded[down], rounded[:, across]), size)
            poly = (coef_b * rounded.astype(f32) + coef_c * square).astype(bf16)
            beside = jnp.concatenate([poly, poly], axis=1)
            if rest is None:
                rest = poly.astype(f32)
            elif iteration == 1:
                rest = coef_a * rest + power * poly.astype(f32) + dot(poly, rest.astype(bf16))
            else:
                below = jnp.concatenate(two(rest), axis=0)
                rest = coef_a * rest + power * poly.astype(f32) + dot(beside, below)
            power = power * coef_a
            if iteration < ITERS - 1:
                left = coef_a * gram + dot(beside, jnp.concatenate(two(gram), axis=0))
                halves = jnp.concatenate(two(left), axis=1)
                twice = jnp.concatenate([poly, poly], axis=0)
                gram = symmetric(
                    lambda down, across: coef_a * left[down, across] + dot(halves[down], twice[:, across]), size
                )
        scale = scale * math.sqrt(full_width)
        high, low = two(rest * scale)
        for i in range(groups):
            factor_ref[i, :rows, :] = high[i * rows : (i + 1) * rows]
            factor_ref[i, rows:, :] = low[i * rows : (i + 1) * rows]
        alpha_ref[...] = jnp.broadcast_to(scale * power, alpha_ref.shape)

    outs = [
        jax.ShapeDtypeStruct((size, width), bf16),
        jax.ShapeDtypeStruct((groups, 2 * rows, size), bf16),
        jax.ShapeDtypeStruct((8, LANES), f32),
    ]
    return call(body, outs, [*sums, *parts], in_vmem(len(sums) + groups), after, name="chain")


def apply_rows(index, factor_ref, alpha_ref, stacks, out_ref):
    rows = factor_ref.shape[1] // 2
    height = out_ref.shape[0]
    left = factor_ref[index]
    own = slice(index * rows, (index + 1) * rows)
    first = 0
    for stack_ref in stacks:
        for at in range(0, stack_ref.shape[1], TILE):
            to = slice(at, min(at + TILE, stack_ref.shape[1]))
            both = dot(left, stack_ref[:, to])
            result = both[:rows] + both[rows:] + alpha_ref[0:1, 0:1] * stack_ref[own, to].astype(f32)
            out_ref[:, first + to.start : first + to.stop] = result[:height].astype(bf16)
        first += stack_ref.shape[1]


def rows_of(factor, alpha, stacks, index, after):
    def body(factor_ref, alpha_ref, *refs):
        apply_rows(index, factor_ref, alpha_ref, refs[:-1], refs[-1])

    outs = [jax.ShapeDtypeStruct((factor.shape[1] // 2, sum(s.shape[1] for s in stacks)), bf16)]
    return call(body, outs, [factor, alpha, *stacks], in_vmem(2 + len(stacks)), after, name=f"rows{index}")[0]


def gate(after, name):
    def body(out_ref):
        out_ref[...] = jnp.zeros_like(out_ref)

    return call(body, [jax.ShapeDtypeStruct((8, LANES), f32)], [], [], after, name=name)[0]


def own_or_received(owners, own, received, cap, after):
    def body(own_ref, *refs):
        *inputs, out_ref = refs
        mine = lax.axis_index("fsdp") == owners + lax.rem(lax.axis_index("rep"), 2)

        @pl.when(mine)
        def _():
            for row in range(0, cap, 16):
                to = slice(row, min(row + 16, cap))
                out_ref[to, :] = own_ref[to, :]

        @pl.when(jnp.logical_not(mine))
        def _():
            for row in range(0, cap, 16):
                to = slice(row, min(row + 16, cap))
                total = None
                for came in inputs:
                    value = came[to, :]
                    total = value if total is None else total + value
                out_ref[to, :] = total

    outs = [jax.ShapeDtypeStruct((cap, own.shape[1]), bf16)]
    specs = in_vmem(1 + len(received))
    return call(body, outs, [own, *received], specs, after, hold=False, name="last")[0]


def per_device(groups, replicas, gradients, momentum, offsets):
    _, mats, cap, width = gradients.shape
    padded = -(-cap // 16) * 16
    bits = [1 << i for i in range(replicas.bit_length() - 1)]

    def swap(value, bit):
        pairs = [(f * replicas + r, f * replicas + (r ^ bit)) for f in range(groups) for r in range(replicas)]
        return lax.ppermute(value, AXES, pairs)

    def owner(r):
        return (groups - 1) // 2 + r % 2

    def others(r):
        return sorted((f for f in range(groups) if f != owner(r)), key=lambda f: -abs(f - owner(r)))

    def to_owner(value, k):
        pairs = [(others(r)[k] * replicas + r, owner(r) * replicas + r) for r in range(replicas)]
        return lax.ppermute(value, AXES, pairs)

    def from_owner(value, k):
        pairs = [(owner(r) * replicas + r, others(r)[k] * replicas + r) for r in range(replicas)]
        return lax.ppermute(value, AXES, pairs)

    flat = jnp.transpose(gradients[0], (1, 0, 2)).reshape(cap * mats, width)
    linear = momentum[0].reshape(cap * (width // LANES), LANES)

    chunks, first = [], 0
    for share in SHARES:
        wide = width // sum(SHARES) * share
        chunks.append((first, wide))
        first += wide
    orders = [bits[1:], bits[1:][::-1]]
    last = ()

    def split_piece(first, wide, apart):
        nonlocal last
        half = wide // 2
        terms, plans = [], []
        for at in (0, half) if apart else (0,):
            keep, send = split(flat, mats, cap, padded, first + at, half if apart else wide, last)
            last = (keep,)
            terms += [keep, swap(send, bits[0])]
        for side in range(2):
            sources = (2 * side, 0) if apart else (0, side * half)
            plans.append(
                {
                    2 * i: [(first + side * half, half, [(sources[0] + t, i, sources[1]) for t in range(2)])]
                    for i in range(mats // 2)
                }
            )
        return terms, plans

    def halve(level, terms, plans, apart):
        nonlocal last
        moving = [[j for j in plan if j & order[level]] for plan, order in zip(plans, orders)]
        wanted = [[[(w, parts) for _, w, parts in plan[j]] for j in away] for plan, away in zip(plans, moving)]
        name = f"fold{level}_{plans[0][0][0][0]}"
        if apart:
            sends = []
            for side in range(2):
                used = sorted({t for segments in wanted[side] for _, parts in segments for t, _, _ in parts})
                own = [
                    [(w, [(used.index(t), p, at) for t, p, at in parts]) for w, parts in segments]
                    for segments in wanted[side]
                ]
                sends += fold([terms[t] for t in used], [own], padded, last, f"{name}_{side}")
                last = (sends[-1],)
        else:
            sends = fold(terms, wanted, padded, last, name)
            last = (sends[0],)
        for side, away in enumerate(moving):
            bit = orders[side][level]
            terms.append(swap(sends[side], bit))
            for place, j in enumerate(away):
                at = 0
                for _, segment, parts in plans[side][j ^ bit]:
                    parts.append((len(terms) - 1, place, at))
                    at += segment
                del plans[side][j]

    means, held = [], []

    def finish(chunk, terms, plans):
        nonlocal last
        segments = [segment for plan in plans for segment in plan[0]]
        own, mean = nesterov(offsets, linear, terms, segments, *chunk, cap, padded, replicas, last)
        last = (own,)
        means.append(mean)
        held.append([own] + [to_owner(own, k) for k in range(groups - 1)])

    levels = len(bits) - 1
    work, arrived, reached = {}, {}, [0] * len(chunks)

    def halve_next(chunk):
        level = reached[chunk]
        halve(level, *work[chunk], False)
        arrived[chunk, level] = tuple(work[chunk][0][-2:])
        reached[chunk] += 1

    for kind, chunk, *more in STEPS:
        if more and isinstance(more[-1], tuple):
            last += arrived.get(more[-1], ())
        if kind == "S":
            work[chunk] = split_piece(*chunks[chunk], False)
        elif kind == "H" and more[0] < levels:
            halve_next(chunk)
        elif kind == "N":
            while reached[chunk] < levels:
                halve_next(chunk)
            finish(chunks[chunk], *work[chunk])
    kept_state = keep_state(offsets, linear, means, cap, last)
    kept_there = pltpu.with_memory_space_constraint(kept_state, pltpu.HBM)
    stacks, sums = [], []
    for parts in held[:-1]:
        stack, partial = gram(parts, (kept_there,), f"gram{len(sums)}")
        stacks.append(stack)
        sums.append(partial)
    stack, factor, alpha = chain(width, sums, held[-1], ())
    stacks.append(stack)
    back = []
    last = ()
    for k in range(groups - 1):
        result = rows_of(factor, alpha, stacks, k + 1, last)
        last = (result,)
        back.append(from_owner(result, k))
    results = last
    last = ()
    for k, came in enumerate(back[:-1]):
        last = (gate((came, *last), f"gate{k}"),)
    own = rows_of(factor, alpha, stacks, 0, results)
    update = own_or_received((groups - 1) // 2, own, back, cap, last)
    return (kept_state.reshape(1, cap, width), update[None])


def solution(mesh):
    placed = (P("rep", None, "fsdp", None), P("rep", "fsdp", None), P("rep", None))
    return jax.shard_map(
        functools.partial(per_device, mesh.shape["fsdp"], mesh.shape["rep"]),
        mesh=mesh,
        in_specs=placed,
        out_specs=(P("rep", "fsdp", None), P("rep", "fsdp", None)),
        check_vma=False,
    )
```

```python
import functools
import math

import jax
import jax.numpy as jnp
from jax import lax
from jax.experimental import pallas as pl
from jax.experimental.pallas import tpu as pltpu
from jax.sharding import PartitionSpec as P

ITERS = 3
SHARES = (7, 7)
STEPS = (('S', 0), ('S', 1), ('H', 0, 0), ('H', 1, 0), ('H', 0, 1), ('H', 1, 1), ('N', 0), ('N', 1))

momentum_rate = 0.95
coef_a = 3.4445
coef_b = -4.775
coef_c = 2.0315

AXES = ("fsdp", "rep")
VMEM_LIMIT = 24 * 1024 * 1024
LANES = 128
TILE = 256
BESIDE = {'gate0': 1, 'gate1': 1, 'nest0': 8.7, 'nest1792': 8.7}
bf16 = jnp.bfloat16
f32 = jnp.float32


def dot(left, right):
    return jnp.dot(left, right, preferred_element_type=f32)


def two(value):
    high = value.astype(bf16)
    return high, (value - high.astype(f32)).astype(bf16)


def in_vmem(count):
    return [pl.BlockSpec(memory_space=pltpu.VMEM)] * count


def in_smem(count):
    return [pl.BlockSpec(memory_space=pltpu.SMEM)] * count


def call(body, outs, inputs, specs, after=(), scratch=(), hold=True, name="step"):
    count = len(inputs)

    def kernel(*refs):
        body(*refs[:count], *refs[count + len(after) :])

    return pl.pallas_call(
        kernel,
        out_shape=tuple(pltpu.VMEM(o.shape, o.dtype) if hold else o for o in outs),
        in_specs=list(specs) + [pl.BlockSpec(memory_space=pl.ANY)] * len(after),
        out_specs=tuple(in_vmem(len(outs))),
        scratch_shapes=list(scratch),
        name=name,
        compiler_params=pltpu.CompilerParams(vmem_limit_bytes=VMEM_LIMIT),
        cost_estimate=pl.CostEstimate(flops=max(1, int(BESIDE.get(name, 0) * 1.15e9)), bytes_accessed=1, transcendentals=0),
    )(*inputs, *after)


def split(flat, mats, cap, padded, first, width, after):
    half = mats // 2
    rows = min(TILE // mats, cap)
    size = rows * mats
    blocks = -(-cap // rows)
    starts = [min(block * rows, cap - rows) for block in range(blocks)]

    def body(x_ref, keep_ref, send_ref, held_ref, sems):
        copies = [
            pltpu.make_async_copy(
                x_ref.at[start * mats : start * mats + size, first : first + width], held_ref.at[i], sems.at[i]
            )
            for i, start in enumerate(starts)
        ]
        for copy in copies:
            copy.start()
        me = lax.axis_index("rep")
        out_row = lax.broadcasted_iota(jnp.int32, (size, 1), 0)
        in_row = lax.broadcasted_iota(jnp.int32, (size, size), 1)
        place = out_row // rows
        within = out_row - place * rows
        kept = place < half
        order = jnp.where(kept, place, place - half)
        reverse = jnp.zeros_like(order)
        high = half.bit_length() - 1
        for bit in range(high):
            reverse = reverse + ((order >> bit) & 1) * (1 << (high - 1 - bit))
        odd = lax.rem(me, 2)
        turned = jnp.where(kept, odd, 1 - odd) == 1
        j = 2 * jnp.where(turned, reverse, order) + jnp.where(kept, 0, 1)
        matrix = jnp.bitwise_xor(j, me)
        chosen = {}
        for block, start in enumerate(starts):
            shift = block * rows - start
            if shift not in chosen:
                source = jnp.where(within < rows - shift, (within + shift) * mats + matrix, -1)
                chosen[shift] = jnp.where(in_row == source, 1.0, 0.0).astype(bf16)
        for block, start in enumerate(starts):
            copies[block].wait()
            for at in range(0, width, TILE):
                wide = min(TILE, width - at)
                moved = dot(chosen[block * rows - start], held_ref[block, :, at : at + wide])
                moved = moved.reshape(mats, rows, wide)
                here = min(rows, padded - block * rows)
                to = slice(block * rows, block * rows + here)
                keep_ref[:, to, at : at + wide] = moved[:half, :here].astype(bf16)
                send_ref[:, to, at : at + wide] = moved[half:, :here].astype(bf16)
        if blocks * rows < padded:
            rest = padded - blocks * rows
            keep_ref[:, blocks * rows :, :] = jnp.zeros((half, rest, width), bf16)
            send_ref[:, blocks * rows :, :] = jnp.zeros((half, rest, width), bf16)

    out = jax.ShapeDtypeStruct((half, padded, width), bf16)
    return call(
        body,
        [out, out],
        [pltpu.with_memory_space_constraint(flat, pltpu.HBM)],
        [pl.BlockSpec(memory_space=pltpu.HBM)],
        after,
        [pltpu.VMEM((blocks, size, width), bf16), pltpu.SemaphoreType.DMA((blocks,))],
        name=f"split{first}",
    )


def added(inputs, parts, rows, width):
    total = None
    for term, place, at in parts:
        value = inputs[term][place, rows, at : at + width].astype(f32)
        total = value if total is None else total + value
    return total


def fold(terms, plans, padded, after, name):
    def body(*refs):
        inputs, outs = refs[: len(terms)], refs[len(terms) :]
        for out, plan in zip(outs, plans):
            for row in range(0, padded, 16):
                to = slice(row, row + 16)
                for i, segments in enumerate(plan):
                    at = 0
                    for width, parts in segments:
                        out[i, to, at : at + width] = added(inputs, parts, to, width).astype(bf16)
                        at += width

    outs = [jax.ShapeDtypeStruct((len(plan), padded, sum(w for w, _ in plan[0])), bf16) for plan in plans]
    return call(body, outs, terms, in_vmem(len(terms)), after, name=name)


def linear_rows(ref, row, cap, blocks, block):
    here = max(0, min(8, cap - row))
    found = []
    if here:
        found.append(ref[pl.ds(row * blocks + block, here, stride=blocks), :])
    if here < 8:
        found.append(jnp.zeros((8 - here, LANES), f32))
    return found[0] if len(found) == 1 else jnp.concatenate(found, axis=0)


def live_count(offsets_ref):
    device = lax.axis_index("fsdp")
    return offsets_ref[0, device + 1] - offsets_ref[0, device]


def nesterov(offsets, linear, terms, segments, first, wide, cap, padded, replicas, after):
    blocks = linear.shape[0] // cap

    def body(*refs):
        offsets_ref, linear_ref, *inputs = refs[: 2 + len(terms)]
        out_ref, mean_ref = refs[2 + len(terms) :]
        count = live_count(offsets_ref)
        for row in range(0, padded, 16):
            slot = lax.broadcasted_iota(jnp.int32, (16, LANES), 0) + row
            to = slice(row, row + 16)
            for start, width, parts in segments:
                for column in range(0, width, LANES):
                    here = [(term, place, at + column) for term, place, at in parts]
                    mean = added(inputs, here, to, LANES) * (1.0 / replicas)
                    block = (start + column) // LANES
                    old = jnp.concatenate(
                        [linear_rows(linear_ref, row + i, cap, blocks, block) for i in (0, 8)], axis=0
                    )
                    new = momentum_rate * old + mean
                    value = jnp.where(slot < count, mean + momentum_rate * new, 0.0)
                    at = start + column - first
                    out_ref[to, at : at + LANES] = value.astype(bf16)
                    mean_ref[to, at : at + LANES] = mean

    outs = [jax.ShapeDtypeStruct((padded, wide), bf16), jax.ShapeDtypeStruct((padded, wide), f32)]
    specs = in_smem(1) + in_vmem(1 + len(terms))
    return call(body, outs, [offsets, linear, *terms], specs, after, name=f"nest{first}")


def keep_state(offsets, linear, means, cap, after):
    blocks = linear.shape[0] // cap

    def body(offsets_ref, linear_ref, *refs):
        inputs, out_ref = refs[:-1], refs[-1]
        count = live_count(offsets_ref)
        for row in range(0, cap, 8):
            here = min(8, cap - row)
            slot = lax.broadcasted_iota(jnp.int32, (here, LANES), 0) + row
            first = 0
            for mean_ref in inputs:
                for column in range(0, mean_ref.shape[1], LANES):
                    at = pl.ds(row * blocks + (first + column) // LANES, here, stride=blocks)
                    new = momentum_rate * linear_ref[at, :] + mean_ref[
                        row : row + here, column : column + LANES
                    ]
                    out_ref[at, :] = jnp.where(slot < count, new, 0.0)
                first += mean_ref.shape[1]

    outs = [jax.ShapeDtypeStruct(linear.shape, f32)]
    specs = in_smem(1) + in_vmem(1 + len(means))
    return call(body, outs, [offsets, linear, *means], specs, after, hold=False, name="keep")[0]


def symmetric(block, size):
    if size <= TILE or size % LANES:
        return block(slice(0, size), slice(0, size))
    left = block(slice(0, size), slice(0, TILE))
    corner = block(slice(TILE, size), slice(TILE, size))
    top = jnp.concatenate([left[:TILE], left[TILE:].T], axis=1)
    return jnp.concatenate([top, jnp.concatenate([left[TILE:], corner], axis=1)], axis=0)


def gram_of(parts, stack_ref):
    rows = parts[0].shape[0]
    for i, part in enumerate(parts):
        stack_ref[i * rows : (i + 1) * rows, :] = part[...]

    def block(down, across):
        return lax.dot_general(
            stack_ref[down, :], stack_ref[across, :], (((1,), (1,)), ((), ())), preferred_element_type=f32
        )

    return symmetric(block, len(parts) * rows)


def gram(parts, after, name):
    size, width = len(parts) * parts[0].shape[0], parts[0].shape[1]

    def body(*refs):
        *inputs, stack_ref, out_ref = refs
        out_ref[...] = gram_of(inputs, stack_ref)

    outs = [jax.ShapeDtypeStruct((size, width), bf16), jax.ShapeDtypeStruct((size, size), f32)]
    return call(body, outs, parts, in_vmem(len(parts)), after, name=name)


def chain(full_width, sums, parts, after):
    groups = len(parts)
    rows, width = parts[0].shape
    size = groups * rows

    def body(*refs):
        earlier, inputs = refs[: len(sums)], refs[len(sums) : -3]
        stack_ref, factor_ref, alpha_ref = refs[-3:]
        gram = gram_of(inputs, stack_ref)
        for earlier_ref in earlier:
            gram = gram + earlier_ref[...]
        diagonal = lax.broadcasted_iota(jnp.int32, (size, size), 0) == lax.broadcasted_iota(
            jnp.int32, (size, size), 1
        )
        trace = jnp.sum(jnp.where(diagonal, gram, 0.0), keepdims=True)
        scale = 1.0 / (jnp.sqrt(trace) + 1e-07)
        gram = (gram * scale) * scale
        rest = None
        power = 1.0
        for iteration in range(ITERS):
            rounded = gram.astype(bf16)
            square = symmetric(lambda down, across: dot(rounded[down], rounded[:, across]), size)
            poly = (coef_b * rounded.astype(f32) + coef_c * square).astype(bf16)
            beside = jnp.concatenate([poly, poly], axis=1)
            if rest is None:
                rest = poly.astype(f32)
            elif iteration == 1:
                rest = coef_a * rest + power * poly.astype(f32) + dot(poly, rest.astype(bf16))
            else:
                below = jnp.concatenate(two(rest), axis=0)
                rest = coef_a * rest + power * poly.astype(f32) + dot(beside, below)
            power = power * coef_a
            if iteration < ITERS - 1:
                left = coef_a * gram + dot(beside, jnp.concatenate(two(gram), axis=0))
                halves = jnp.concatenate(two(left), axis=1)
                twice = jnp.concatenate([poly, poly], axis=0)
                gram = symmetric(
                    lambda down, across: coef_a * left[down, across] + dot(halves[down], twice[:, across]), size
                )
        scale = scale * math.sqrt(full_width)
        high, low = two(rest * scale)
        for i in range(groups):
            factor_ref[i, :rows, :] = high[i * rows : (i + 1) * rows]
            factor_ref[i, rows:, :] = low[i * rows : (i + 1) * rows]
        alpha_ref[...] = jnp.broadcast_to(scale * power, alpha_ref.shape)

    outs = [
        jax.ShapeDtypeStruct((size, width), bf16),
        jax.ShapeDtypeStruct((groups, 2 * rows, size), bf16),
        jax.ShapeDtypeStruct((8, LANES), f32),
    ]
    return call(body, outs, [*sums, *parts], in_vmem(len(sums) + groups), after, name="chain")


def apply_rows(index, factor_ref, alpha_ref, stacks, out_ref):
    rows = factor_ref.shape[1] // 2
    height = out_ref.shape[0]
    even, odd = index
    block = jnp.where(lax.rem(lax.axis_index("rep"), 2) == 0, even, odd)
    left = factor_ref[block]
    own = pl.ds(pl.multiple_of(block * rows, rows), rows)
    first = 0
    for stack_ref in stacks:
        for at in range(0, stack_ref.shape[1], TILE):
            to = slice(at, min(at + TILE, stack_ref.shape[1]))
            both = dot(left, stack_ref[:, to])
            result = both[:rows] + both[rows:] + alpha_ref[0:1, 0:1] * stack_ref[own, to].astype(f32)
            out_ref[:, first + to.start : first + to.stop] = result[:height].astype(bf16)
        first += stack_ref.shape[1]


def rows_of(factor, alpha, stacks, index, after):
    def body(factor_ref, alpha_ref, *refs):
        apply_rows(index, factor_ref, alpha_ref, refs[:-1], refs[-1])

    outs = [jax.ShapeDtypeStruct((factor.shape[1] // 2, sum(s.shape[1] for s in stacks)), bf16)]
    return call(body, outs, [factor, alpha, *stacks], in_vmem(2 + len(stacks)), after, name=f"rows{index[0]}")[0]


def gate(after, name):
    def body(out_ref):
        out_ref[...] = jnp.zeros_like(out_ref)

    return call(body, [jax.ShapeDtypeStruct((8, LANES), f32)], [], [], after, name=name)[0]


def own_or_received(owners, own, received, cap, after):
    def body(own_ref, *refs):
        *inputs, out_ref = refs
        mine = lax.axis_index("fsdp") == owners + lax.rem(lax.axis_index("rep"), 2)

        @pl.when(mine)
        def _():
            for row in range(0, cap, 16):
                to = slice(row, min(row + 16, cap))
                out_ref[to, :] = own_ref[to, :]

        @pl.when(jnp.logical_not(mine))
        def _():
            for row in range(0, cap, 16):
                to = slice(row, min(row + 16, cap))
                total = None
                for came in inputs:
                    value = came[to, :]
                    total = value if total is None else total + value
                out_ref[to, :] = total

    outs = [jax.ShapeDtypeStruct((cap, own.shape[1]), bf16)]
    specs = in_vmem(1 + len(received))
    return call(body, outs, [own, *received], specs, after, hold=False, name="last")[0]


def per_device(groups, replicas, gradients, momentum, offsets):
    _, mats, cap, width = gradients.shape
    padded = -(-cap // 16) * 16
    bits = [1 << i for i in range(replicas.bit_length() - 1)]

    def swap(value, bit):
        def partner(r):
            if r % 2 and bit > 1:
                return r ^ bits[1:][::-1][bits.index(bit) - 1]
            return r ^ bit

        pairs = [(f * replicas + r, f * replicas + partner(r)) for f in range(groups) for r in range(replicas)]
        return lax.ppermute(value, AXES, pairs)

    def owner(r):
        return (groups - 1) // 2 + r % 2

    def others(r):
        return sorted((f for f in range(groups) if f != owner(r)), key=lambda f: -abs(f - owner(r)))

    def to_owner(value, k):
        pairs = [(others(r)[k] * replicas + r, owner(r) * replicas + r) for r in range(replicas)]
        return lax.ppermute(value, AXES, pairs)

    def from_owner(value, k):
        pairs = [(owner(r) * replicas + r, returns(r)[k] * replicas + r) for r in range(replicas)]
        return lax.ppermute(value, AXES, pairs)

    def returns(r):
        return sorted(others(r), key=lambda f: f > 0)

    def place(r, k):
        return others(r).index(returns(r)[k]) + 1

    flat = jnp.transpose(gradients[0], (1, 0, 2)).reshape(cap * mats, width)
    linear = momentum[0].reshape(cap * (width // LANES), LANES)

    chunks, first = [], 0
    for share in SHARES:
        wide = width // sum(SHARES) * share
        chunks.append((first, wide))
        first += wide
    orders = [bits[1:], bits[1:][::-1]]
    last = ()

    def split_piece(first, wide, apart):
        nonlocal last
        half = wide // 2
        terms, plans = [], []
        for at in (0, half) if apart else (0,):
            keep, send = split(flat, mats, cap, padded, first + at, half if apart else wide, last)
            last = (keep,)
            terms += [keep, swap(send, bits[0])]
        for side in range(2):
            sources = (2 * side, 0) if apart else (0, side * half)
            plans.append(
                {
                    2 * i: [(first + side * half, half, [(sources[0] + t, i, sources[1]) for t in range(2)])]
                    for i in range(mats // 2)
                }
            )
        return terms, plans

    def halve(level, terms, plans, apart):
        nonlocal last
        moving = [[j for j in plan if j & order[level]] for plan, order in zip(plans, orders)]
        wanted = [[[(w, parts) for _, w, parts in plan[j]] for j in away] for plan, away in zip(plans, moving)]
        name = f"fold{level}_{plans[0][0][0][0]}"
        if apart:
            sends = []
            for side in range(2):
                used = sorted({t for segments in wanted[side] for _, parts in segments for t, _, _ in parts})
                own = [
                    [(w, [(used.index(t), p, at) for t, p, at in parts]) for w, parts in segments]
                    for segments in wanted[side]
                ]
                sends += fold([terms[t] for t in used], [own], padded, last, f"{name}_{side}")
                last = (sends[-1],)
        else:
            sends = fold(terms, wanted, padded, last, name)
            last = (sends[0],)
        for side, away in enumerate(moving):
            bit = orders[side][level]
            terms.append(swap(sends[side], bit))
            for place, j in enumerate(away):
                at = 0
                for _, segment, parts in plans[side][j ^ bit]:
                    parts.append((len(terms) - 1, place, at))
                    at += segment
                del plans[side][j]

    means, held = [], []

    def finish(chunk, terms, plans):
        nonlocal last
        segments = [segment for plan in plans for segment in plan[0]]
        own, mean = nesterov(offsets, linear, terms, segments, *chunk, cap, padded, replicas, last)
        last = (own,)
        means.append(mean)
        held.append([own] + [to_owner(own, k) for k in range(groups - 1)])

    levels = len(bits) - 1
    work, arrived, reached = {}, {}, [0] * len(chunks)

    def halve_next(chunk):
        level = reached[chunk]
        halve(level, *work[chunk], False)
        arrived[chunk, level] = tuple(work[chunk][0][-2:])
        reached[chunk] += 1

    for kind, chunk, *more in STEPS:
        if more and isinstance(more[-1], tuple):
            last += arrived.get(more[-1], ())
        if kind == "S":
            work[chunk] = split_piece(*chunks[chunk], False)
        elif kind == "H" and more[0] < levels:
            halve_next(chunk)
        elif kind == "N":
            while reached[chunk] < levels:
                halve_next(chunk)
            finish(chunks[chunk], *work[chunk])
    kept_state = keep_state(offsets, linear, means, cap, last)
    kept_there = pltpu.with_memory_space_constraint(kept_state, pltpu.HBM)
    stacks, sums = [], []
    for parts in held[:-1]:
        stack, partial = gram(parts, (kept_there,), f"gram{len(sums)}")
        stacks.append(stack)
        sums.append(partial)
    stack, factor, alpha = chain(width, sums, held[-1], ())
    stacks.append(stack)
    back = []
    last = ()
    for k in range(groups - 1):
        result = rows_of(factor, alpha, stacks, (place(0, k), place(1, k)), last)
        last = (result,)
        back.append(from_owner(result, k))
    results = last
    last = ()
    for k, came in enumerate(back[:-1]):
        last = (gate((came, *last), f"gate{k}"),)
    own = rows_of(factor, alpha, stacks, (0, 0), results)
    update = own_or_received((groups - 1) // 2, own, back, cap, last)
    return (kept_state.reshape(1, cap, width), update[None])


def solution(mesh):
    placed = (P("rep", None, "fsdp", None), P("rep", "fsdp", None), P("rep", None))
    return jax.shard_map(
        functools.partial(per_device, mesh.shape["fsdp"], mesh.shape["rep"]),
        mesh=mesh,
        in_specs=placed,
        out_specs=(P("rep", "fsdp", None), P("rep", "fsdp", None)),
        check_vma=False,
    )
```
